512 devices in a mesh: patch: 128 (over x_hi, y, z), head: 4 (over x_lo, core).
Axes of the slice: x: 4 (x_hi: 2, x_lo: 2; x = x_hi * 2 + x_lo), y: 4, z: 16, core: 2. Of those that a mesh axis runs over, the one named last changes fastest.
Arguments:
- latents: bfloat16 [16384, 1536], P('patch', 'head'), may hold values from -6 to 6
- timestep: int32 [1], replicated, may hold values from 0 to 999
- conv_weight: float32 [3, 1536], P(None, 'head'), may hold values from -3 to 3
- norm_gain: float32 [1536], replicated, may hold values from 0.1 to 1.9
- ada_gain: float32 [1536], replicated, may hold values from -4 to 4
- w_query: bfloat16 [1536, 2560], P(None, 'head'), may hold values from -0.15625 to 0.15625
- w_kv: bfloat16 [2, 1536, 512], P(None, None, 'head'), may hold values from -0.375 to 0.375
- w_out: bfloat16 [2560, 1536], P('head'), may hold values from -0.125 to 0.125
- stale_kv: bfloat16 [2, 16384, 512], P(None, 'patch', 'head'), may hold values from -280 to 280
Outputs:
- denoised: bfloat16 [16384, 1536], P('patch', 'head')
- fresh_kv: bfloat16 [2, 16384, 512], P(None, 'patch', 'head')
The draws below stay inside these ranges and needn't reach their ends.
All inputs are finite; a program needn't handle non-finite values.
Results may differ from the reference program's by a relative error of at most 0.024.
The reference program's roundings to bfloat16 on the way count: a program that leaves them out, or rounds other values in their place, can miss the bound.
Values may be sent and summed in bfloat16 or wider, within the bound.
No kernel may reach another device: no remote copies, remote signals or barrier semaphores. Data moves between devices by JAX's collectives and lax.ppermute only.
A program may use at most 64 MiB of HBM per device.

```python
import math
import jax
import jax.numpy as jnp
from jax import lax

D = 1536
H = 20
HD = 128
KVH = 4
TOK_DEV = 128
TOKENS = 16384
N_PATCH = 128


def draw_stale_kv(key, part):
    key = jax.random.fold_in(key, 11)
    key_a = jax.random.fold_in(key, 0)
    column_scale = jnp.array([4.0, 2.0], jnp.float32).reshape(2, 1, 1)
    base = jax.random.normal(key_a, (2, TOKENS, KVH * HD), jnp.float32)
    values = jnp.clip(base * column_scale, -20.0, 20.0)
    return values.astype(jnp.bfloat16)


def level_of(key, shape, cuts, low, high):
    loudness, own = 1.0, jax.random.fold_in(key, 6)
    for dim, blocks in cuts:
        draws = jnp.exp(jax.random.uniform(jax.random.fold_in(own, dim), (blocks,), jnp.float32, low / len(cuts), high / len(cuts)))
        loudness = loudness * jnp.repeat(draws, shape[dim] // blocks).reshape([-1 if axis == dim else 1 for axis in range(len(shape))])
    return loudness


def scatter_about(rng, extent, scale, most, pieces=(), kind=jnp.bfloat16):
    entries = scale * jax.random.normal(rng, extent, jnp.float32)
    if pieces:
        entries = entries * level_of(rng, extent, pieces, -0.22, 0.18)
    return jnp.clip(entries, -most, most).astype(kind)


def setup_inputs(seed: int = 0) -> dict:
    seeds = jax.random.split(jax.random.key(seed), 10)
    return {
        "latents": scatter_about(seeds[0], (TOKENS, D), 1.0, 6.0, ((0, 128), (1, 4))),
        "timestep": jax.random.randint(seeds[1], (1,), 0, 1000).astype(jnp.int32),
        "conv_weight": scatter_about(seeds[2], (3, D), 0.5, 3.0, ((1, 4),), jnp.float32),
        "norm_gain": jnp.clip(1.0 + 0.18 * jax.random.normal(seeds[3], (D,), jnp.float32), 0.1, 1.9),
        "ada_gain": scatter_about(seeds[4], (D,), 1.0, 4.0, (), jnp.float32),
        "w_query": scatter_about(seeds[5], (D, H * HD), D ** -0.5, 0.15625, ((1, 4),)),
        "w_kv": scatter_about(seeds[6], (2, D, KVH * HD), (D // 6) ** -0.5, 0.375, ((2, 4),)),
        "w_out": scatter_about(seeds[7], (H * HD, D), (H * HD) ** -0.5, 0.125, ((0, 4),)),
        "stale_kv": draw_stale_kv(jax.random.fold_in(seeds[9], 71), 0),
    }


def embed(timestep, width):
    half_width = width // 2
    channel = jnp.arange(width, dtype=jnp.int32)
    freq_row = jnp.exp(-math.log(10000.0) * (channel % half_width).astype(jnp.float32) / half_width)
    phases = timestep.astype(jnp.float32)[0] * freq_row
    return jnp.where(channel < half_width, jnp.sin(phases), jnp.cos(phases))

def patch_attention(queries, fresh_kv, stale_kv, patch_at):
    begin_at = (patch_at * TOK_DEV).astype(jnp.int32)
    per_group = H // KVH
    query_blk = lax.dynamic_slice_in_dim(queries, begin_at, TOK_DEV, 0)
    query_blk = lax.optimization_barrier(query_blk).astype(jnp.float32).reshape(TOK_DEV, KVH, per_group, HD)
    fresh_blk = lax.dynamic_slice_in_dim(fresh_kv, begin_at, TOK_DEV, 1)
    table = lax.dynamic_update_slice_in_dim(stale_kv, fresh_blk, begin_at, 1)
    table = lax.optimization_barrier(table).astype(jnp.float32).reshape(2, TOKENS, KVH, HD)
    scores = jnp.einsum('tgjd,ngd->gjtn', query_blk, table[0]) * (1.0 / math.sqrt(HD))
    top_score = lax.optimization_barrier(jnp.max(scores, axis=-1, keepdims=True))
    weights = jnp.exp(scores - top_score)
    total = lax.optimization_barrier(jnp.sum(weights, axis=-1))
    rounded = lax.optimization_barrier(weights.astype(jnp.bfloat16)).astype(jnp.float32)
    mixed = jnp.einsum('gjtn,ngd->tgjd', rounded, table[1])
    mixed = mixed / jnp.transpose(total, (2, 0, 1))[..., None]
    return mixed.reshape(TOK_DEV, H * HD).astype(jnp.bfloat16)

def reference(latents, timestep, conv_weight, norm_gain, ada_gain, w_query, w_kv, w_out, stale_kv):
    source = latents.astype(jnp.float32)
    padded = jnp.pad(source, ((1, 1), (0, 0)))
    stem_out = (source + conv_weight[0] * padded[:-2] + conv_weight[1] * source + conv_weight[2] * padded[2:]).astype(jnp.bfloat16)
    stem_f = lax.optimization_barrier(stem_out).astype(jnp.float32)
    inv_rms = lax.rsqrt(lax.optimization_barrier(jnp.mean(stem_f * stem_f, axis=1, keepdims=True)) + 1e-06)
    modulate = norm_gain * (1.0 + 0.3 * ada_gain * embed(timestep, D))
    normed = (stem_f * inv_rms * modulate).astype(jnp.bfloat16)
    queries = jnp.dot(normed, w_query, preferred_element_type=jnp.float32).astype(jnp.bfloat16)
    fresh_kv = jnp.stack([jnp.dot(normed, w_kv[0], preferred_element_type=jnp.float32), jnp.dot(normed, w_kv[1], preferred_element_type=jnp.float32)]).astype(jnp.bfloat16)
    patch_ids = jnp.arange(N_PATCH, dtype=jnp.int32)
    attended = lax.map(lambda patch_at: patch_attention(queries, fresh_kv, stale_kv, patch_at), patch_ids)
    attended = attended.reshape(TOKENS, H * HD)
    update = jnp.dot(attended, w_out, preferred_element_type=jnp.float32)
    denoised = (stem_f + update).astype(jnp.bfloat16)
    return (denoised, fresh_kv)
```

```python
import functools
import math

import jax
import jax.numpy as jnp
from jax import lax
from jax.experimental import pallas as pl
from jax.experimental.pallas import tpu as pltpu
from jax.sharding import Mesh, PartitionSpec as P

EPS_NORM = 1e-06
HD = 128
GROUP = 5
TOK = 128
PEERS = 8
RING = 16
KEYS = RING * TOK
COLS = GROUP * HD
PAY = COLS + 128
LOG2_SCALE = math.log2(math.e) / math.sqrt(HD)
NT = (((1,), (1,)), ((), ()))
VMEM_LIMIT = 48 * 2**20


def embed(timestep, width):
    half_width = width // 2
    channel = jnp.arange(width, dtype=jnp.int32)
    freq_row = jnp.exp(-math.log(10000.0) * (channel % half_width).astype(jnp.float32) / half_width)
    phases = timestep.astype(jnp.float32)[0] * freq_row
    return jnp.where(channel < half_width, jnp.sin(phases), jnp.cos(phases))


def from_z(value, offset):
    return lax.ppermute(value, "z", [((i + offset) % RING, i) for i in range(RING)])


def gather_ring(kv):
    own = kv[None]
    up = from_z(own, 1)
    down = from_z(own, -1)
    parts = [up, down]
    up = from_z(jnp.concatenate([own, up]), 2)
    down = from_z(jnp.concatenate([own, down]), -2)
    parts += [up, down]
    for _ in range(2):
        up, down = from_z(up, 2), from_z(down, -2)
        parts += [up, down]
    parts.append(from_z(up[1:], 1))
    return parts


def attend_kernel(me_ref, q_ref, fresh_ref, *refs):
    del me_ref
    parts, (o_ref, k_s, v_s, s_s) = refs[:-4], refs[-4:]
    step = pl.program_id(0)

    @pl.when(step == 0)
    def _():
        row = 0
        for part in parts:
            for b in range(part.shape[0]):
                k_s[row : row + TOK, :] = part[b, 0]
                v_s[row : row + TOK, :HD] = part[b, 1]
                row += TOK
        v_s[:, HD:] = jnp.ones((KEYS, HD), jnp.bfloat16)

    @pl.when(step == PEERS - 1)
    def _():
        k_s[:TOK, :] = fresh_ref[0]
        v_s[:TOK, :HD] = fresh_ref[1]

    lane = lax.broadcasted_iota(jnp.int32, (TOK, 128), 1)
    extra = jnp.zeros((TOK, 128), jnp.float32)
    chunk = 512
    for h in range(GROUP):
        q = q_ref[0, :, h * HD : (h + 1) * HD]
        top = None
        for c in range(0, KEYS, chunk):
            s = lax.dot_general(q, k_s[c : c + chunk, :], NT, preferred_element_type=jnp.float32)
            s_s[h, :, c : c + chunk] = s
            t = functools.reduce(jnp.maximum, [s[:, j : j + 128] for j in range(0, chunk, 128)])
            top = t if top is None else jnp.maximum(top, t)
        top = jnp.max(top, axis=1, keepdims=True)
        acc = None
        for c in range(0, KEYS, chunk):
            p = jnp.exp2((s_s[h, :, c : c + chunk] - top) * LOG2_SCALE).astype(jnp.bfloat16)
            a = jnp.dot(p, v_s[c : c + chunk, :], preferred_element_type=jnp.float32)
            acc = a if acc is None else acc + a
        total = acc[:, HD:]
        o_ref[0, :, h * HD : (h + 1) * HD] = (acc[:, :HD] / total).astype(jnp.bfloat16)
        lse = top * LOG2_SCALE + jnp.log2(total)
        hi = lse.astype(jnp.bfloat16).astype(jnp.float32)
        mid = (lse - hi).astype(jnp.bfloat16).astype(jnp.float32)
        low = lse - hi - mid
        for n, term in enumerate((hi, mid, low)):
            extra = jnp.where(lane == 3 * h + n, term, extra)
    o_ref[0, :, COLS:] = extra.astype(jnp.bfloat16)


def attend(me, queries, fresh, parts):
    whole = lambda a: pl.BlockSpec(a.shape, lambda i, me_ref: (0,) * a.ndim)
    at = lambda i, me_ref: ((me_ref[0] + 1 + i) % PEERS, 0, 0)
    return pl.pallas_call(
        attend_kernel,
        grid_spec=pltpu.PrefetchScalarGridSpec(
            num_scalar_prefetch=1,
            grid=(PEERS,),
            in_specs=[pl.BlockSpec((1, TOK, COLS), at), whole(fresh)] + [whole(p) for p in parts],
            out_specs=pl.BlockSpec((1, TOK, PAY), at),
            scratch_shapes=[
                pltpu.VMEM((KEYS, HD), jnp.bfloat16),
                pltpu.VMEM((KEYS, 2 * HD), jnp.bfloat16),
                pltpu.VMEM((GROUP, TOK, KEYS), jnp.float32),
            ],
        ),
        out_shape=jax.ShapeDtypeStruct((PEERS, TOK, PAY), jnp.bfloat16),
        compiler_params=pltpu.CompilerParams(vmem_limit_bytes=VMEM_LIMIT),
        cost_estimate=pl.CostEstimate(flops=6 * 10**9, bytes_accessed=4 * 10**6, transcendentals=10**7),
    )(me, queries, fresh, *parts)


def merge_kernel(parts_ref, w_ref, o_ref):
    cols = []
    for h in range(GROUP):
        lses = []
        for j in range(PEERS):
            e = parts_ref[j, :, COLS:].astype(jnp.float32)
            lses.append(e[:, 3 * h : 3 * h + 1] + e[:, 3 * h + 1 : 3 * h + 2] + e[:, 3 * h + 2 : 3 * h + 3])
        top = functools.reduce(jnp.maximum, lses)
        total, acc = 0.0, 0.0
        for j in range(PEERS):
            w = jnp.exp2(lses[j] - top)
            total += w
            acc += w * parts_ref[j, :, h * HD : (h + 1) * HD].astype(jnp.float32)
        cols.append((acc / total).astype(jnp.bfloat16))
    attended = jnp.concatenate(cols, axis=1)
    o_ref[...] = jnp.dot(attended, w_ref[...], preferred_element_type=jnp.float32).astype(jnp.bfloat16)


def merge(parts, w_out):
    return pl.pallas_call(
        merge_kernel,
        out_shape=jax.ShapeDtypeStruct((TOK, w_out.shape[1]), jnp.bfloat16),
        compiler_params=pltpu.CompilerParams(vmem_limit_bytes=VMEM_LIMIT),
    )(parts, w_out)


def per_device(latents, timestep, conv_weight, norm_gain, ada_gain, w_query, w_kv, w_out, stale_kv):
    width = latents.shape[1]
    line = ("xh", "y", "z")
    n = 128
    up = [(i, i + 1) for i in range(n - 1)]
    before = lax.ppermute(latents[-1:], line, up)
    after = lax.ppermute(latents[:1], line, [(j, i) for i, j in up])
    kv_parts = [stale_kv[None]] + gather_ring(stale_kv)
    rimmed = jnp.concatenate([before, latents, after], axis=0).astype(jnp.float32)
    centre = rimmed[1:-1]
    stem = (
        centre + conv_weight[0] * rimmed[:-2] + conv_weight[1] * centre + conv_weight[2] * rimmed[2:]
    ).astype(jnp.bfloat16)
    gathered = lax.all_gather(stem, "head", axis=1, tiled=True).astype(jnp.float32)
    inv_rms = lax.rsqrt(jnp.mean(gathered * gathered, axis=1, keepdims=True) + EPS_NORM)
    modulate = norm_gain * (1.0 + 0.3 * ada_gain * embed(timestep, gathered.shape[1]))
    normed = (gathered * inv_rms * modulate).astype(jnp.bfloat16)
    queries = jnp.dot(normed, w_query, preferred_element_type=jnp.float32).astype(jnp.bfloat16)
    fresh = jnp.einsum("td,kde->kte", normed, w_kv, preferred_element_type=jnp.float32).astype(jnp.bfloat16)
    spread = jnp.broadcast_to(queries[None], (PEERS, TOK, COLS))
    all_queries = lax.all_to_all(spread, ("xh", "y"), 0, 0)
    me = lax.axis_index(("xh", "y")).astype(jnp.int32).reshape(1)
    partial = attend(me, all_queries, fresh, kv_parts)
    partial = lax.all_to_all(partial, ("xh", "y"), 0, 0)
    terms = merge(partial, w_out)
    terms = terms.reshape(TOK, 4, width).transpose(1, 0, 2)
    terms = lax.all_to_all(terms, "head", 0, 0)
    update = jnp.sum(terms.astype(jnp.float32), axis=0)
    denoised = (stem.astype(jnp.float32) + update).astype(jnp.bfloat16)
    return (denoised, fresh)


def solution(mesh):
    fine = Mesh(mesh.devices.reshape(2, 4, RING, 4), ("xh", "y", "z", "head"))
    patch = ("xh", "y", "z")
    return jax.shard_map(
        per_device,
        mesh=fine,
        in_specs=(
            P(patch, "head"),
            P(),
            P(None, "head"),
            P(),
            P(),
            P(None, "head"),
            P(None, None, "head"),
            P("head", None),
            P(None, patch, "head"),
        ),
        out_specs=(P(patch, "head"), P(None, patch, "head")),
        check_vma=False,
    )
```

```python
import functools
import math

import jax
import jax.numpy as jnp
from jax import lax
from jax.experimental import pallas as pl
from jax.experimental.pallas import tpu as pltpu
from jax.sharding import Mesh, PartitionSpec as P

EPS_NORM = 1e-06
HD = 128
GROUP = 5
TOK = 128
PEERS = 4
ROWS = 320
PLANE = ("xh", "zl")
COLS = GROUP * HD
PAY = COLS + 128
LOG2_SCALE = math.log2(math.e) / math.sqrt(HD)
NT = (((1,), (1,)), ((), ()))
VMEM_LIMIT = 48 * 2**20


def embed(timestep, width):
    half_width = width // 2
    channel = jnp.arange(width, dtype=jnp.int32)
    freq_row = jnp.exp(-math.log(10000.0) * (channel % half_width).astype(jnp.float32) / half_width)
    phases = timestep.astype(jnp.float32)[0] * freq_row
    return jnp.where(channel < half_width, jnp.sin(phases), jnp.cos(phases))


def swap(value, turn):
    n = lax.axis_size("zh")
    pairs = []
    for i in range(turn, n + turn, 2):
        j = (i + 1) % n
        pairs += [(i, j), (j, i)]
    return lax.ppermute(value, "zh", pairs)


def flip(value, bits):
    return lax.ppermute(value, PLANE, [(i, i ^ bits) for i in range(PEERS)])


def attend_kernel(where_ref, *refs):
    qs, (near_ref, far_ref, fresh_ref, o_ref, k_s, v_s, s_s) = refs[:PEERS], refs[PEERS:]
    keys = k_s.shape[0]
    row = 0
    for ref in (near_ref, far_ref):
        for y in range(ref.shape[0]):
            for b in range(ref.shape[1]):
                k_s[row : row + TOK, :] = ref[y, b, 0]
                v_s[row : row + TOK, :HD] = ref[y, b, 1]
                row += TOK
    v_s[:, HD:] = jnp.ones((keys, HD), jnp.bfloat16)
    for bits in range(PEERS - 1, -1, -1):
        if bits == 0:
            rows = pl.ds(pl.multiple_of(where_ref[1] * TOK, TOK), TOK)
            k_s[rows, :] = fresh_ref[0]
            v_s[rows, :HD] = fresh_ref[1]
        attend_patch(qs[bits], o_ref.at[where_ref[0] ^ bits], k_s, v_s, s_s)


def attend_patch(q_ref, o_ref, k_s, v_s, s_s):
    keys = k_s.shape[0]
    q = jnp.concatenate([q_ref[:, h * HD : (h + 1) * HD] for h in range(GROUP)], axis=0)
    chunk = 512

    def scores(r):
        top = None
        for c in range(0, keys, chunk):
            s = lax.dot_general(q[r : r + ROWS], k_s[c : c + chunk, :], NT, preferred_element_type=jnp.float32)
            s_s[r : r + ROWS, c : c + chunk] = s
            t = functools.reduce(jnp.maximum, [s[:, j : j + 128] for j in range(0, chunk, 128)])
            top = t if top is None else jnp.maximum(top, t)
        return jnp.max(top, axis=1, keepdims=True)

    def mix(r, top):
        acc = None
        for c in range(0, keys, chunk):
            p = jnp.exp2((s_s[r : r + ROWS, c : c + chunk] - top) * LOG2_SCALE).astype(jnp.bfloat16)
            a = jnp.dot(p, v_s[c : c + chunk, :], preferred_element_type=jnp.float32)
            acc = a if acc is None else acc + a
        total = acc[:, HD:]
        return acc[:, :HD] / total, top * LOG2_SCALE + jnp.log2(total)

    starts = list(range(0, COLS, ROWS))
    tops, mixed = [scores(0)], []
    for n, r in enumerate(starts):
        if n + 1 < len(starts):
            tops.append(scores(starts[n + 1]))
        mixed.append(mix(r, tops[n]))
    out, lses = (jnp.concatenate([m[i] for m in mixed], axis=0) for i in range(2))
    lane = lax.broadcasted_iota(jnp.int32, (TOK, 128), 1)
    extra = jnp.zeros((TOK, 128), jnp.float32)
    for h in range(GROUP):
        rows = slice(h * TOK, (h + 1) * TOK)
        o_ref[:, h * HD : (h + 1) * HD] = out[rows].astype(jnp.bfloat16)
        lse = lses[rows]
        hi = lse.astype(jnp.bfloat16).astype(jnp.float32)
        mid = (lse - hi).astype(jnp.bfloat16).astype(jnp.float32)
        low = lse - hi - mid
        for n, term in enumerate((hi, mid, low)):
            extra = jnp.where(lane == 3 * h + n, term, extra)
    o_ref[:, COLS:] = extra.astype(jnp.bfloat16)


def attend(where, queries, near, far, fresh):
    keys = TOK * (math.prod(near.shape[:2]) + math.prod(far.shape[:2]))
    vmem = pl.BlockSpec(memory_space=pltpu.VMEM)
    return pl.pallas_call(
        attend_kernel,
        in_specs=[pl.BlockSpec(memory_space=pltpu.SMEM)] + [vmem] * (PEERS + 3),
        out_specs=vmem,
        scratch_shapes=[
            pltpu.VMEM((keys, HD), jnp.bfloat16),
            pltpu.VMEM((keys, 2 * HD), jnp.bfloat16),
            pltpu.VMEM((COLS, keys), jnp.float32),
        ],
        out_shape=jax.ShapeDtypeStruct((PEERS, TOK, PAY), jnp.bfloat16),
        compiler_params=pltpu.CompilerParams(vmem_limit_bytes=VMEM_LIMIT),
        cost_estimate=pl.CostEstimate(
            flops=15 * 10**9, bytes_accessed=4 * 10**6, transcendentals=PEERS * COLS * keys
        ),
    )(where, *queries, near, far, fresh)


def copies_kernel(n_parts, *refs):
    parts, out_ref = refs[:n_parts], refs[-1]
    for j in range(out_ref.shape[0]):
        row = 0
        for part in parts:
            n = part.shape[0]
            out_ref[j, row : row + n] = part[...]
            row += n


def spread(parts, n, behind):
    blocks = sum(p.shape[0] for p in parts)
    vmem = pl.BlockSpec(memory_space=pltpu.VMEM)
    return pl.pallas_call(
        functools.partial(copies_kernel, len(parts)),
        in_specs=[vmem] * len(parts) + [pl.BlockSpec(memory_space=pl.ANY)],
        out_specs=vmem,
        out_shape=jax.ShapeDtypeStruct((n, blocks) + parts[0].shape[1:], jnp.bfloat16),
        compiler_params=pltpu.CompilerParams(vmem_limit_bytes=VMEM_LIMIT),
        cost_estimate=pl.CostEstimate(flops=10**5, bytes_accessed=10**6, transcendentals=0),
    )(*parts, behind)


def stem_kernel(x_ref, before_ref, after_ref, w_ref, stem_ref):
    x = x_ref[...].astype(jnp.float32)
    row = lax.broadcasted_iota(jnp.int32, x.shape, 0)
    prev = jnp.where(row == 0, before_ref[...].astype(jnp.float32), pltpu.roll(x, 1, 0))
    follow = jnp.where(row == TOK - 1, after_ref[...].astype(jnp.float32), pltpu.roll(x, TOK - 1, 0))
    stem = x + w_ref[0:1, :] * prev + w_ref[1:2, :] * x + w_ref[2:3, :] * follow
    stem_ref[...] = stem.astype(jnp.bfloat16)


def stem_of(latents, before, after, conv_weight):
    vmem = pl.BlockSpec(memory_space=pltpu.VMEM)
    return pl.pallas_call(
        stem_kernel,
        in_specs=[vmem] * 4,
        out_specs=vmem,
        out_shape=jax.ShapeDtypeStruct(latents.shape, jnp.bfloat16),
        compiler_params=pltpu.CompilerParams(vmem_limit_bytes=VMEM_LIMIT),
        cost_estimate=pl.CostEstimate(flops=10**6, bytes_accessed=10**6, transcendentals=0),
    )(latents, before, after, conv_weight)


def project_kernel(x_ref, mod_ref, wq_ref, wkv_ref, q_ref, fresh_ref):
    x = x_ref[...].astype(jnp.float32)
    inv = lax.rsqrt(jnp.mean(x * x, axis=1, keepdims=True) + EPS_NORM)
    normed = (x * inv * mod_ref[...]).astype(jnp.bfloat16)
    q_ref[...] = jnp.dot(normed, wq_ref[...], preferred_element_type=jnp.float32).astype(jnp.bfloat16)
    for i in range(2):
        fresh_ref[i] = jnp.dot(normed, wkv_ref[i], preferred_element_type=jnp.float32).astype(jnp.bfloat16)


def project(x, mod, w_query, w_kv):
    vmem = pl.BlockSpec(memory_space=pltpu.VMEM)
    return pl.pallas_call(
        project_kernel,
        in_specs=[vmem] * 4,
        out_shape=[
            jax.ShapeDtypeStruct((TOK, COLS), jnp.bfloat16),
            jax.ShapeDtypeStruct((2, TOK, HD), jnp.bfloat16),
        ],
        compiler_params=pltpu.CompilerParams(vmem_limit_bytes=VMEM_LIMIT),
        cost_estimate=pl.CostEstimate(flops=4 * 10**8, bytes_accessed=5 * 10**6, transcendentals=0),
    )(x, mod, w_query, w_kv)


def merge_kernel(parts_ref, w_ref, o_ref):
    cols = []
    for h in range(GROUP):
        lses = []
        for j in range(PEERS):
            e = parts_ref[j, :, COLS:].astype(jnp.float32)
            lses.append(e[:, 3 * h : 3 * h + 1] + e[:, 3 * h + 1 : 3 * h + 2] + e[:, 3 * h + 2 : 3 * h + 3])
        top = functools.reduce(jnp.maximum, lses)
        total, acc = 0.0, 0.0
        for j in range(PEERS):
            w = jnp.exp2(lses[j] - top)
            total += w
            acc += w * parts_ref[j, :, h * HD : (h + 1) * HD].astype(jnp.float32)
        cols.append((acc / total).astype(jnp.bfloat16))
    attended = jnp.concatenate(cols, axis=1)
    o_ref[...] = jnp.dot(attended, w_ref[...], preferred_element_type=jnp.float32).astype(jnp.bfloat16)


def merge(parts, w_out):
    return pl.pallas_call(
        merge_kernel,
        out_shape=jax.ShapeDtypeStruct((TOK, w_out.shape[1]), jnp.bfloat16),
        compiler_params=pltpu.CompilerParams(vmem_limit_bytes=VMEM_LIMIT),
    )(parts, w_out)


def per_device(latents, timestep, conv_weight, norm_gain, ada_gain, w_query, w_kv, w_out, stale_kv):
    width = latents.shape[1]
    line = ("xh", "y", "zh", "zl")
    n = 128
    up = [(i, i + 1) for i in range(n - 1)]
    before = lax.ppermute(latents[-1:], line, up)
    after = lax.ppermute(latents[:1], line, [(j, i) for i, j in up])
    own = stale_kv[None]
    got = [swap(own, 0)]
    stem = stem_of(latents, before, after, conv_weight)
    got.append(swap(spread([own] + got, 1, stem)[0], 1))
    gathered = lax.all_gather(stem, "head", axis=1, tiled=True)
    modulate = norm_gain * (1.0 + 0.3 * ada_gain * embed(timestep, gathered.shape[1]))
    near = lax.all_to_all(spread([own] + got, 4, gathered), "y", 0, 0)
    got.append(swap(got[1], 0))
    queries, fresh = project(gathered, modulate[None], w_query, w_kv)
    got.append(swap(spread(got[2:3], 1, queries)[0], 1))
    all_queries = [queries] + [flip(queries, bits) for bits in range(1, PEERS)]
    far = lax.all_to_all(spread(got[2:], 4, all_queries[1]), "y", 0, 0)
    where = jnp.stack([lax.axis_index(PLANE), 4 * lax.axis_index("y")]).astype(jnp.int32)
    partial = attend(where, all_queries, near, far, fresh)
    partial = lax.all_to_all(partial, PLANE, 0, 0)
    terms = merge(partial, w_out)
    terms = terms.reshape(TOK, 4, width).transpose(1, 0, 2)
    terms = lax.all_to_all(terms, "head", 0, 0)
    update = jnp.sum(terms.astype(jnp.float32), axis=0)
    denoised = (stem.astype(jnp.float32) + update).astype(jnp.bfloat16)
    return (denoised, fresh)


def solution(mesh):
    fine = Mesh(mesh.devices.reshape(2, 4, 8, 2, 4), ("xh", "y", "zh", "zl", "head"))
    patch = ("xh", "y", "zh", "zl")
    return jax.shard_map(
        per_device,
        mesh=fine,
        in_specs=(
            P(patch, "head"),
            P(),
            P(None, "head"),
            P(),
            P(),
            P(None, "head"),
            P(None, None, "head"),
            P("head", None),
            P(None, patch, "head"),
        ),
        out_specs=(P(patch, "head"), P(None, patch, "head")),
        check_vma=False,
    )
```

```python
import functools
import math

import jax
import jax.numpy as jnp
from jax import lax
from jax.experimental import pallas as pl
from jax.experimental.pallas import tpu as pltpu
from jax.sharding import Mesh, PartitionSpec as P

EPS_NORM = 1e-06
HD = 128
GROUP = 5
TOK = 128
PEERS = 4
ROWS = 320
PLANE = ("xh", "zl")
COLS = GROUP * HD
PAY = COLS + 128
LOG2_SCALE = math.log2(math.e) / math.sqrt(HD)
NT = (((1,), (1,)), ((), ()))
VMEM_LIMIT = 48 * 2**20


def embed(timestep, width):
    half_width = width // 2
    channel = jnp.arange(width, dtype=jnp.int32)
    freq_row = jnp.exp(-math.log(10000.0) * (channel % half_width).astype(jnp.float32) / half_width)
    phases = timestep.astype(jnp.float32)[0] * freq_row
    return jnp.where(channel < half_width, jnp.sin(phases), jnp.cos(phases))


def swap(value, turn):
    n = lax.axis_size("zh")
    pairs = []
    for i in range(turn, n + turn, 2):
        j = (i + 1) % n
        pairs += [(i, j), (j, i)]
    return lax.ppermute(value, "zh", pairs)


def flip(value, bits):
    return lax.ppermute(value, PLANE, [(i, i ^ bits) for i in range(PEERS)])


def attend_kernel(where_ref, *refs):
    qs, (near_ref, far_ref, fresh_ref, o_ref, k_s, v_s, s_s) = refs[:PEERS], refs[PEERS:]
    keys = k_s.shape[0]
    row = 0
    for ref in (near_ref, far_ref):
        for y in range(ref.shape[0]):
            for b in range(ref.shape[1]):
                k_s[row : row + TOK, :] = ref[y, b, 0]
                v_s[row : row + TOK, :HD] = ref[y, b, 1]
                row += TOK
    v_s[:, HD:] = jnp.ones((keys, HD), jnp.bfloat16)
    for bits in range(PEERS - 1, -1, -1):
        if bits == 0:
            rows = pl.ds(pl.multiple_of(where_ref[1] * TOK, TOK), TOK)
            k_s[rows, :] = fresh_ref[0]
            v_s[rows, :HD] = fresh_ref[1]
        attend_patch(qs[bits], o_ref.at[where_ref[0] ^ bits], k_s, v_s, s_s)


def attend_patch(q_ref, o_ref, k_s, v_s, s_s):
    keys = k_s.shape[0]
    q = jnp.concatenate([q_ref[:, h * HD : (h + 1) * HD] for h in range(GROUP)], axis=0)
    chunk = 512

    def scores(r):
        top = None
        for c in range(0, keys, chunk):
            s = lax.dot_general(q[r : r + ROWS], k_s[c : c + chunk, :], NT, preferred_element_type=jnp.float32)
            s_s[r : r + ROWS, c : c + chunk] = s
            t = functools.reduce(jnp.maximum, [s[:, j : j + 128] for j in range(0, chunk, 128)])
            top = t if top is None else jnp.maximum(top, t)
        return jnp.max(top, axis=1, keepdims=True)

    def mix(r, top):
        acc = None
        for c in range(0, keys, chunk):
            p = jnp.exp2((s_s[r : r + ROWS, c : c + chunk] - top) * LOG2_SCALE).astype(jnp.bfloat16)
            a = jnp.dot(p, v_s[c : c + chunk, :], preferred_element_type=jnp.float32)
            acc = a if acc is None else acc + a
        total = acc[:, HD:]
        return acc[:, :HD] / total, top * LOG2_SCALE + jnp.log2(total)

    starts = list(range(0, COLS, ROWS))
    tops, mixed = [scores(0)], []
    for n, r in enumerate(starts):
        if n + 1 < len(starts):
            tops.append(scores(starts[n + 1]))
        mixed.append(mix(r, tops[n]))
    out, lses = (jnp.concatenate([m[i] for m in mixed], axis=0) for i in range(2))
    lane = lax.broadcasted_iota(jnp.int32, (TOK, 128), 1)
    extra = jnp.zeros((TOK, 128), jnp.float32)
    for h in range(GROUP):
        rows = slice(h * TOK, (h + 1) * TOK)
        o_ref[:, h * HD : (h + 1) * HD] = out[rows].astype(jnp.bfloat16)
        lse = lses[rows]
        hi = lse.astype(jnp.bfloat16).astype(jnp.float32)
        mid = (lse - hi).astype(jnp.bfloat16).astype(jnp.float32)
        low = lse - hi - mid
        for n, term in enumerate((hi, mid, low)):
            extra = jnp.where(lane == 3 * h + n, term, extra)
    o_ref[:, COLS:] = extra.astype(jnp.bfloat16)


def attend(where, queries, near, far, fresh):
    keys = TOK * (math.prod(near.shape[:2]) + math.prod(far.shape[:2]))
    vmem = pl.BlockSpec(memory_space=pltpu.VMEM)
    return pl.pallas_call(
        attend_kernel,
        in_specs=[pl.BlockSpec(memory_space=pltpu.SMEM)] + [vmem] * (PEERS + 3),
        out_specs=vmem,
        scratch_shapes=[
            pltpu.VMEM((keys, HD), jnp.bfloat16),
            pltpu.VMEM((keys, 2 * HD), jnp.bfloat16),
            pltpu.VMEM((COLS, keys), jnp.float32),
        ],
        out_shape=jax.ShapeDtypeStruct((PEERS, TOK, PAY), jnp.bfloat16),
        compiler_params=pltpu.CompilerParams(vmem_limit_bytes=VMEM_LIMIT),
        cost_estimate=pl.CostEstimate(
            flops=15 * 10**9, bytes_accessed=4 * 10**6, transcendentals=PEERS * COLS * keys
        ),
    )(where, *queries, near, far, fresh)


def copies_kernel(n_parts, *refs):
    parts, out_ref = refs[:n_parts], refs[-1]
    for j in range(out_ref.shape[0]):
        row = 0
        for part in parts:
            n = part.shape[0]
            out_ref[j, row : row + n] = part[...]
            row += n


def spread(parts, n, *behind):
    blocks = sum(p.shape[0] for p in parts)
    vmem = pl.BlockSpec(memory_space=pltpu.VMEM)
    return pl.pallas_call(
        functools.partial(copies_kernel, len(parts)),
        in_specs=[vmem] * len(parts) + [pl.BlockSpec(memory_space=pl.ANY)] * len(behind),
        out_specs=vmem,
        out_shape=jax.ShapeDtypeStruct((n, blocks) + parts[0].shape[1:], jnp.bfloat16),
        compiler_params=pltpu.CompilerParams(vmem_limit_bytes=VMEM_LIMIT),
        cost_estimate=pl.CostEstimate(flops=10**5, bytes_accessed=10**6, transcendentals=0),
    )(*parts, *behind)


def stem_kernel(x_ref, before_ref, after_ref, w_ref, stem_ref):
    x = x_ref[...].astype(jnp.float32)
    row = lax.broadcasted_iota(jnp.int32, x.shape, 0)
    prev = jnp.where(row == 0, before_ref[...].astype(jnp.float32), pltpu.roll(x, 1, 0))
    follow = jnp.where(row == TOK - 1, after_ref[...].astype(jnp.float32), pltpu.roll(x, TOK - 1, 0))
    stem = x + w_ref[0:1, :] * prev + w_ref[1:2, :] * x + w_ref[2:3, :] * follow
    stem_ref[...] = stem.astype(jnp.bfloat16)


def stem_of(latents, before, after, conv_weight):
    vmem = pl.BlockSpec(memory_space=pltpu.VMEM)
    return pl.pallas_call(
        stem_kernel,
        in_specs=[vmem] * 4,
        out_specs=vmem,
        out_shape=jax.ShapeDtypeStruct(latents.shape, jnp.bfloat16),
        compiler_params=pltpu.CompilerParams(vmem_limit_bytes=VMEM_LIMIT),
        cost_estimate=pl.CostEstimate(flops=10**6, bytes_accessed=10**6, transcendentals=0),
    )(latents, before, after, conv_weight)


def project_kernel(x_ref, mod_ref, wq_ref, wkv_ref, q_ref, fresh_ref):
    x = x_ref[...].astype(jnp.float32)
    inv = lax.rsqrt(jnp.mean(x * x, axis=1, keepdims=True) + EPS_NORM)
    normed = (x * inv * mod_ref[...]).astype(jnp.bfloat16)
    q_ref[...] = jnp.dot(normed, wq_ref[...], preferred_element_type=jnp.float32).astype(jnp.bfloat16)
    for i in range(2):
        fresh_ref[i] = jnp.dot(normed, wkv_ref[i], preferred_element_type=jnp.float32).astype(jnp.bfloat16)


def project(x, mod, w_query, w_kv):
    vmem = pl.BlockSpec(memory_space=pltpu.VMEM)
    return pl.pallas_call(
        project_kernel,
        in_specs=[vmem] * 4,
        out_shape=[
            jax.ShapeDtypeStruct((TOK, COLS), jnp.bfloat16),
            jax.ShapeDtypeStruct((2, TOK, HD), jnp.bfloat16),
        ],
        compiler_params=pltpu.CompilerParams(vmem_limit_bytes=VMEM_LIMIT),
        cost_estimate=pl.CostEstimate(flops=4 * 10**8, bytes_accessed=5 * 10**6, transcendentals=0),
    )(x, mod, w_query, w_kv)


def merge_kernel(parts_ref, w_ref, o_ref):
    cols = []
    for h in range(GROUP):
        lses = []
        for j in range(PEERS):
            e = parts_ref[j, :, COLS:].astype(jnp.float32)
            lses.append(e[:, 3 * h : 3 * h + 1] + e[:, 3 * h + 1 : 3 * h + 2] + e[:, 3 * h + 2 : 3 * h + 3])
        top = functools.reduce(jnp.maximum, lses)
        total, acc = 0.0, 0.0
        for j in range(PEERS):
            w = jnp.exp2(lses[j] - top)
            total += w
            acc += w * parts_ref[j, :, h * HD : (h + 1) * HD].astype(jnp.float32)
        cols.append((acc / total).astype(jnp.bfloat16))
    attended = jnp.concatenate(cols, axis=1)
    o_ref[...] = jnp.dot(attended, w_ref[...], preferred_element_type=jnp.float32).astype(jnp.bfloat16)


def merge(parts, w_out):
    return pl.pallas_call(
        merge_kernel,
        out_shape=jax.ShapeDtypeStruct((TOK, w_out.shape[1]), jnp.bfloat16),
        compiler_params=pltpu.CompilerParams(vmem_limit_bytes=VMEM_LIMIT),
    )(parts, w_out)


def per_device(latents, timestep, conv_weight, norm_gain, ada_gain, w_query, w_kv, w_out, stale_kv):
    width = latents.shape[1]
    line = ("xh", "y", "zh", "zl")
    n = 128
    up = [(i, i + 1) for i in range(n - 1)]
    before = lax.ppermute(latents[-1:], line, up)
    after = lax.ppermute(latents[:1], line, [(j, i) for i, j in up])
    own = stale_kv[None]
    got = [swap(own, 0)]
    stem = stem_of(latents, before, after, conv_weight)
    got.append(swap(spread([own] + got, 1, stem)[0], 1))
    gathered = lax.all_gather(stem, "head", axis=1, tiled=True)
    modulate = norm_gain * (1.0 + 0.3 * ada_gain * embed(timestep, gathered.shape[1]))
    got.append(swap(got[1], 0))
    near = lax.all_to_all(spread([own] + got, 4, gathered), "y", 0, 0)
    queries, fresh = project(gathered, modulate[None], w_query, w_kv)
    all_queries = [queries] + [flip(queries, bits) for bits in range(1, PEERS)]
    far = lax.all_to_all(spread([swap(got[2], 1)], 4, all_queries[1], all_queries[2]), "y", 0, 0)
    where = jnp.stack([lax.axis_index(PLANE), 6 * lax.axis_index("y")]).astype(jnp.int32)
    partial = attend(where, all_queries, near, far, fresh)
    partial = lax.all_to_all(partial, PLANE, 0, 0)
    terms = merge(partial, w_out)
    terms = terms.reshape(TOK, 4, width).transpose(1, 0, 2)
    terms = lax.all_to_all(terms, "head", 0, 0)
    update = jnp.sum(terms.astype(jnp.float32), axis=0)
    denoised = (stem.astype(jnp.float32) + update).astype(jnp.bfloat16)
    return (denoised, fresh)


def solution(mesh):
    fine = Mesh(mesh.devices.reshape(2, 4, 8, 2, 4), ("xh", "y", "zh", "zl", "head"))
    patch = ("xh", "y", "zh", "zl")
    return jax.shard_map(
        per_device,
        mesh=fine,
        in_specs=(
            P(patch, "head"),
            P(),
            P(None, "head"),
            P(),
            P(),
            P(None, "head"),
            P(None, None, "head"),
            P("head", None),
            P(None, patch, "head"),
        ),
        out_specs=(P(patch, "head"), P(None, patch, "head")),
        check_vma=False,
    )
```

```python
import functools
import math

import jax
import jax.numpy as jnp
from jax import lax
from jax.experimental import pallas as pl
from jax.experimental.pallas import tpu as pltpu
from jax.sharding import Mesh, PartitionSpec as P

EPS_NORM = 1e-06
HD = 128
GROUP = 5
TOK = 128
PEERS = 4
ROWS = 320
PLANE = ("xh", "zl")
COLS = GROUP * HD
PAY = COLS + 128
LOG2_SCALE = math.log2(math.e) / math.sqrt(HD)
NT = (((1,), (1,)), ((), ()))
VMEM_LIMIT = 48 * 2**20


def embed(timestep, width):
    half_width = width // 2
    channel = jnp.arange(width, dtype=jnp.int32)
    freq_row = jnp.exp(-math.log(10000.0) * (channel % half_width).astype(jnp.float32) / half_width)
    phases = timestep.astype(jnp.float32)[0] * freq_row
    return jnp.where(channel < half_width, jnp.sin(phases), jnp.cos(phases))


def swap(value, turn):
    n = lax.axis_size("zh")
    pairs = []
    for i in range(turn, n + turn, 2):
        j = (i + 1) % n
        pairs += [(i, j), (j, i)]
    return lax.ppermute(value, "zh", pairs)


def flip(value, bits):
    return lax.ppermute(value, PLANE, [(i, i ^ bits) for i in range(PEERS)])


def attend_kernel(where_ref, *refs):
    qs, (near_ref, far_ref, fresh_ref, o_ref, k_s, v_s, s_s) = refs[:PEERS], refs[PEERS:]
    keys = k_s.shape[0]
    row = 0
    for ref in (near_ref, far_ref):
        for y in range(ref.shape[0]):
            for b in range(ref.shape[1]):
                k_s[row : row + TOK, :] = ref[y, b, 0]
                v_s[row : row + TOK, :HD] = ref[y, b, 1]
                row += TOK
    v_s[:, HD:] = jnp.ones((keys, HD), jnp.bfloat16)
    for bits in range(PEERS - 1, -1, -1):
        if bits == 0:
            rows = pl.ds(pl.multiple_of(where_ref[1] * TOK, TOK), TOK)
            k_s[rows, :] = fresh_ref[0]
            v_s[rows, :HD] = fresh_ref[1]
        attend_patch(qs[bits], o_ref.at[where_ref[0] ^ bits], k_s, v_s, s_s)


def attend_patch(q_ref, o_ref, k_s, v_s, s_s):
    keys = k_s.shape[0]
    q = jnp.concatenate([q_ref[:, h * HD : (h + 1) * HD] for h in range(GROUP)], axis=0)
    chunk = 512

    def scores(r):
        top = None
        for c in range(0, keys, chunk):
            s = lax.dot_general(q[r : r + ROWS], k_s[c : c + chunk, :], NT, preferred_element_type=jnp.float32)
            s_s[r : r + ROWS, c : c + chunk] = s
            t = functools.reduce(jnp.maximum, [s[:, j : j + 128] for j in range(0, chunk, 128)])
            top = t if top is None else jnp.maximum(top, t)
        return jnp.max(top, axis=1, keepdims=True)

    def mix(r, top):
        acc = None
        for c in range(0, keys, chunk):
            p = jnp.exp2((s_s[r : r + ROWS, c : c + chunk] - top) * LOG2_SCALE).astype(jnp.bfloat16)
            a = jnp.dot(p, v_s[c : c + chunk, :], preferred_element_type=jnp.float32)
            acc = a if acc is None else acc + a
        total = acc[:, HD:]
        return acc[:, :HD] / total, top * LOG2_SCALE + jnp.log2(total)

    starts = list(range(0, COLS, ROWS))
    tops, mixed = [scores(0)], []
    for n, r in enumerate(starts):
        if n + 1 < len(starts):
            tops.append(scores(starts[n + 1]))
        mixed.append(mix(r, tops[n]))
    out, lses = (jnp.concatenate([m[i] for m in mixed], axis=0) for i in range(2))
    lane = lax.broadcasted_iota(jnp.int32, (TOK, 128), 1)
    extra = jnp.zeros((TOK, 128), jnp.float32)
    for h in range(GROUP):
        rows = slice(h * TOK, (h + 1) * TOK)
        o_ref[:, h * HD : (h + 1) * HD] = out[rows].astype(jnp.bfloat16)
        lse = lses[rows]
        hi = lse.astype(jnp.bfloat16).astype(jnp.float32)
        mid = (lse - hi).astype(jnp.bfloat16).astype(jnp.float32)
        low = lse - hi - mid
        for n, term in enumerate((hi, mid, low)):
            extra = jnp.where(lane == 3 * h + n, term, extra)
    o_ref[:, COLS:] = extra.astype(jnp.bfloat16)


def attend(where, queries, near, far, fresh):
    keys = TOK * (math.prod(near.shape[:2]) + math.prod(far.shape[:2]))
    vmem = pl.BlockSpec(memory_space=pltpu.VMEM)
    return pl.pallas_call(
        attend_kernel,
        in_specs=[pl.BlockSpec(memory_space=pltpu.SMEM)] + [vmem] * (PEERS + 3),
        out_specs=vmem,
        scratch_shapes=[
            pltpu.VMEM((keys, HD), jnp.bfloat16),
            pltpu.VMEM((keys, 2 * HD), jnp.bfloat16),
            pltpu.VMEM((COLS, keys), jnp.float32),
        ],
        out_shape=jax.ShapeDtypeStruct((PEERS, TOK, PAY), jnp.bfloat16),
        compiler_params=pltpu.CompilerParams(vmem_limit_bytes=VMEM_LIMIT),
        cost_estimate=pl.CostEstimate(
            flops=15 * 10**9, bytes_accessed=4 * 10**6, transcendentals=PEERS * COLS * keys
        ),
    )(where, *queries, near, far, fresh)


def copies_kernel(n_parts, *refs):
    parts, out_ref = refs[:n_parts], refs[-1]
    for j in range(out_ref.shape[0]):
        row = 0
        for part in parts:
            n = part.shape[0]
            out_ref[j, row : row + n] = part[...]
            row += n


def spread(parts, n, *behind):
    blocks = sum(p.shape[0] for p in parts)
    vmem = pl.BlockSpec(memory_space=pltpu.VMEM)
    return pl.pallas_call(
        functools.partial(copies_kernel, len(parts)),
        in_specs=[vmem] * len(parts) + [pl.BlockSpec(memory_space=pl.ANY)] * len(behind),
        out_specs=vmem,
        out_shape=jax.ShapeDtypeStruct((n, blocks) + parts[0].shape[1:], jnp.bfloat16),
        compiler_params=pltpu.CompilerParams(vmem_limit_bytes=VMEM_LIMIT),
        cost_estimate=pl.CostEstimate(flops=10**5, bytes_accessed=10**6, transcendentals=0),
    )(*parts, *behind)


def stem_kernel(x_ref, before_ref, after_ref, w_ref, stem_ref):
    x = x_ref[...].astype(jnp.float32)
    row = lax.broadcasted_iota(jnp.int32, x.shape, 0)
    prev = jnp.where(row == 0, before_ref[...].astype(jnp.float32), pltpu.roll(x, 1, 0))
    follow = jnp.where(row == TOK - 1, after_ref[...].astype(jnp.float32), pltpu.roll(x, TOK - 1, 0))
    stem = x + w_ref[0:1, :] * prev + w_ref[1:2, :] * x + w_ref[2:3, :] * follow
    stem_ref[...] = stem.astype(jnp.bfloat16)


def stem_of(latents, before, after, conv_weight):
    vmem = pl.BlockSpec(memory_space=pltpu.VMEM)
    return pl.pallas_call(
        stem_kernel,
        in_specs=[vmem] * 4,
        out_specs=vmem,
        out_shape=jax.ShapeDtypeStruct(latents.shape, jnp.bfloat16),
        compiler_params=pltpu.CompilerParams(vmem_limit_bytes=VMEM_LIMIT),
        cost_estimate=pl.CostEstimate(flops=10**6, bytes_accessed=10**6, transcendentals=0),
    )(latents, before, after, conv_weight)


def project_kernel(x_ref, mod_ref, wq_ref, wkv_ref, q_ref, fresh_ref):
    x = x_ref[...].astype(jnp.float32)
    inv = lax.rsqrt(jnp.mean(x * x, axis=1, keepdims=True) + EPS_NORM)
    normed = (x * inv * mod_ref[...]).astype(jnp.bfloat16)
    q_ref[...] = jnp.dot(normed, wq_ref[...], preferred_element_type=jnp.float32).astype(jnp.bfloat16)
    for i in range(2):
        fresh_ref[i] = jnp.dot(normed, wkv_ref[i], preferred_element_type=jnp.float32).astype(jnp.bfloat16)


def project(x, mod, w_query, w_kv):
    vmem = pl.BlockSpec(memory_space=pltpu.VMEM)
    return pl.pallas_call(
        project_kernel,
        in_specs=[vmem] * 4,
        out_shape=[
            jax.ShapeDtypeStruct((TOK, COLS), jnp.bfloat16),
            jax.ShapeDtypeStruct((2, TOK, HD), jnp.bfloat16),
        ],
        compiler_params=pltpu.CompilerParams(vmem_limit_bytes=VMEM_LIMIT),
        cost_estimate=pl.CostEstimate(flops=4 * 10**8, bytes_accessed=5 * 10**6, transcendentals=0),
    )(x, mod, w_query, w_kv)


def merge_kernel(parts_ref, w_ref, o_ref):
    cols = []
    for h in range(GROUP):
        lses = []
        for j in range(PEERS):
            e = parts_ref[j, :, COLS:].astype(jnp.float32)
            lses.append(e[:, 3 * h : 3 * h + 1] + e[:, 3 * h + 1 : 3 * h + 2] + e[:, 3 * h + 2 : 3 * h + 3])
        top = functools.reduce(jnp.maximum, lses)
        total, acc = 0.0, 0.0
        for j in range(PEERS):
            w = jnp.exp2(lses[j] - top)
            total += w
            acc += w * parts_ref[j, :, h * HD : (h + 1) * HD].astype(jnp.float32)
        cols.append((acc / total).astype(jnp.bfloat16))
    attended = jnp.concatenate(cols, axis=1)
    o_ref[...] = jnp.dot(attended, w_ref[...], preferred_element_type=jnp.float32).astype(jnp.bfloat16)


def merge(parts, w_out):
    return pl.pallas_call(
        merge_kernel,
        out_shape=jax.ShapeDtypeStruct((TOK, w_out.shape[1]), jnp.bfloat16),
        compiler_params=pltpu.CompilerParams(vmem_limit_bytes=VMEM_LIMIT),
    )(parts, w_out)


def per_device(latents, timestep, conv_weight, norm_gain, ada_gain, w_query, w_kv, w_out, stale_kv):
    width = latents.shape[1]
    line = ("xh", "y", "zh", "zl")
    n = 128
    up = [(i, i + 1) for i in range(n - 1)]
    before = lax.ppermute(latents[-1:], line, up)
    after = lax.ppermute(latents[:1], line, [(j, i) for i, j in up])
    own = stale_kv[None]
    got = [swap(own, 0)]
    stem = stem_of(latents, before, after, conv_weight)
    got.append(swap(spread([own] + got, 1, stem)[0], 1))
    gathered = lax.all_gather(stem, "head", axis=1, tiled=True)
    modulate = norm_gain * (1.0 + 0.3 * ada_gain * embed(timestep, gathered.shape[1]))
    got.append(swap(got[1], 0))
    near = lax.all_to_all(spread([own] + got, 4, gathered), "y", 0, 0)
    queries, fresh = project(gathered, modulate[None], w_query, w_kv)
    all_queries = [queries] + [flip(queries, bits) for bits in range(1, PEERS)]
    far = lax.all_to_all(spread([swap(got[2], 1)], 4, all_queries[1], all_queries[2], near), "y", 0, 0)
    where = jnp.stack([lax.axis_index(PLANE), 6 * lax.axis_index("y")]).astype(jnp.int32)
    partial = attend(where, all_queries, near, far, fresh)
    partial = lax.all_to_all(partial, PLANE, 0, 0)
    terms = merge(partial, w_out)
    terms = terms.reshape(TOK, 4, width).transpose(1, 0, 2)
    terms = lax.all_to_all(terms, "head", 0, 0)
    update = jnp.sum(terms.astype(jnp.float32), axis=0)
    denoised = (stem.astype(jnp.float32) + update).astype(jnp.bfloat16)
    return (denoised, fresh)


def solution(mesh):
    fine = Mesh(mesh.devices.reshape(2, 4, 8, 2, 4), ("xh", "y", "zh", "zl", "head"))
    patch = ("xh", "y", "zh", "zl")
    return jax.shard_map(
        per_device,
        mesh=fine,
        in_specs=(
            P(patch, "head"),
            P(),
            P(None, "head"),
            P(),
            P(),
            P(None, "head"),
            P(None, None, "head"),
            P("head", None),
            P(None, patch, "head"),
        ),
        out_specs=(P(patch, "head"), P(None, patch, "head")),
        check_vma=False,
    )
```
